32 devices in a mesh: dp: 4 (over y, x), pts: 8 (over z, core).
Axes of the slice: x: 2, y: 2, z: 4, core: 2. Of those that a mesh axis runs over, the one named last changes fastest.
Arguments:
- features: bfloat16 [32768, 256], P(('dp', 'pts')), parts along dimension 0, may hold values from -6 to 6
- tile_slot: int32 [32768], P(('dp', 'pts')), parts along dimension 0, may hold values from 0 to 16383, as said below
- neighbors: int32 [27, 65536], P(None, ('dp', 'pts')), parts along dimension 1, may hold values from 0 to 2304, as said below
- serial: int32 [65536], P(('dp', 'pts')), parts along dimension 0, may hold values from -1 to 8191, as said below
- conv_weight: bfloat16 [27, 256, 256], replicated, may hold values from -0.078125 to 0.078125
- conv_bias: float32 [256], replicated, may hold values from -3 to 3
- cpe_gain: float32 [256], replicated, may hold values from 0.1 to 1.9
- cpe_bias: float32 [256], replicated, may hold values from -3 to 3
- norm_gain: float32 [256], replicated, may hold values from 0.1 to 1.9
- norm_bias: float32 [256], replicated, may hold values from -3 to 3
- qkv_weight: bfloat16 [256, 768], replicated, may hold values from -0.375 to 0.375
- qkv_bias: float32 [768], replicated, may hold values from -50 to 50
- proj_weight: bfloat16 [256, 256], replicated, may hold values from -0.375 to 0.375
- proj_bias: float32 [256], replicated, may hold values from -3 to 3
Outputs:
- output: bfloat16 [32768, 256], P(('dp', 'pts')), parts along dimension 0
The draws below stay inside these ranges and needn't reach their ends.
There are 4 independent parts, one for each index of `dp`. The reference program is written for one: setup_inputs(seed, part) draws one part's arguments, and reference() takes and returns one part's arrays. A program takes and returns all parts, laid end to end along the dimension named above; an argument that names none is the same for every part. Nothing has to cross between parts.
Inputs may be any that keep to these rules, and one draw needn't show every extreme that they name: `tile_slot`: element i gives point i's owner (value // 2048) and slot (value % 2048); values are distinct. An owner holds a first run of its slots and always its last 128 slots; it holds at least 256 slots and some owner holds all 2048. From the 1024 points of one device at most 272 go to one owner, and some device sends exactly 272 to some owner. `neighbors`: entry [k, s] refers to the extended rows of slot s's owner: 0 to 127 are the last 128 slots of the owner before, 128 + j is the owner's own slot j, 2176 + j is slot j of the owner after, 2304 means no neighbour. Entries name held slots only; the first owner never names an owner before and the last none after. Entry 13 of a held slot is the slot itself; all entries of slots no point holds are 2304. `serial`: held slots carry the places 0 to 8191, each once; slots no point holds carry -1. From one owner at most 272 points go to the places of one device (block of 1024 places), and some owner sends exactly 272 to some device.
All inputs are finite; a program needn't handle non-finite values.
Results may differ from the reference program's by a relative error of at most 0.014.
Values may be sent and summed in bfloat16 or wider, within the bound.
A program may use at most 64 MiB of HBM per device.

```python
import jax
import jax.numpy as jnp
from jax import lax

D = 256
HEADS = 16
HD = 16
PATCH = 1024
PTS_DEV = 1024
OWN_CAP = 2048
HALO = 128
EXT_ROWS = 2304
TOKENS = 8192
TILE_ROWS = 16384
N_PTS = 8


def circulant(key, spread):
    key_one, key_two = jax.random.split(key)
    levels = jax.random.randint(key_one, (N_PTS,), 0, spread + 1)
    levels = levels.at[0].set(spread).at[1].set(0)
    rotation = jax.random.randint(key_two, (), 0, N_PTS)
    rotated = (jnp.arange(N_PTS) + rotation) % N_PTS
    return levels[rotated] - levels[(rotated + 1) % N_PTS]


def layout(key):
    mean_share = PTS_DEV // N_PTS
    spread = mean_share // 8
    subkeys = jax.random.split(jax.random.fold_in(key, 7), 12)
    levels = jax.random.randint(subkeys[0], (N_PTS,), mean_share // 4, 3 * mean_share // 4 + 1)
    levels = levels.at[0].set(mean_share).at[1].set(0)
    rotation = jax.random.randint(subkeys[1], (), 0, N_PTS)
    rotated = (jnp.arange(N_PTS) + rotation) % N_PTS
    owner_load = mean_share + levels[rotated] - levels[(rotated + 1) % N_PTS]
    wave_one = circulant(subkeys[2], spread)
    wave_two = circulant(subkeys[3], spread)
    devices = jnp.arange(N_PTS)
    sent_counts = owner_load[None, :] + wave_one[(devices[:, None] - devices[None, :]) % N_PTS]
    moved = owner_load[:, None] + wave_two[(devices[None, :] - devices[:, None]) % N_PTS]
    held_count = N_PTS * owner_load
    return (subkeys, held_count, sent_counts, moved)


def live_order(key, held_count):
    random_bits = jax.random.randint(key, (N_PTS, OWN_CAP), 0, 2 ** 30 // OWN_CAP)
    column = jnp.arange(OWN_CAP)
    scores = jnp.where(column[None, :] < held_count[:, None], random_bits * OWN_CAP + column[None, :], 2 ** 30 + column[None, :])
    return jnp.argsort(scores, axis=1, stable=True).astype(jnp.int32)


def slot_index(live_index, held_count):
    return jnp.where(live_index < held_count - HALO, live_index, OWN_CAP - held_count + live_index)


def draw_tile_slot(key, part):
    subkeys, held_count, sent_counts, moved = layout(key)
    devices = jnp.arange(N_PTS)
    placing = live_order(subkeys[4], held_count)
    before = jnp.cumsum(sent_counts, axis=0) - sent_counts
    upper_ends = jnp.cumsum(sent_counts, axis=1)
    starts = upper_ends - sent_counts
    position = jnp.arange(PTS_DEV)
    owner_of = jnp.sum((position[None, :, None] >= upper_ends[:, None, :]).astype(jnp.int32), axis=2)
    ranking = position[None, :] - jnp.take_along_axis(starts, owner_of, axis=1)
    live_index = jnp.take_along_axis(before, owner_of, axis=1) + ranking
    permuted = placing[owner_of, live_index]
    slot_at = slot_index(permuted, held_count[owner_of])
    entries = owner_of * OWN_CAP + slot_at
    shuffles = jax.vmap(lambda subkey: jax.random.permutation(subkey, PTS_DEV))(jax.random.split(subkeys[5], N_PTS))
    result = jnp.zeros((N_PTS, PTS_DEV), jnp.int32).at[devices[:, None], shuffles].set(entries.astype(jnp.int32))
    return result.reshape(-1).astype(jnp.int32)


def draw_serial(key, part):
    subkeys, held_count, sent_counts, moved = layout(key)
    devices = jnp.arange(N_PTS)
    ordering = live_order(subkeys[6], held_count)
    upper_ends = jnp.cumsum(moved, axis=1)
    starts = upper_ends - moved
    steps_all = jnp.arange(OWN_CAP)
    destination = jnp.sum((steps_all[None, :, None] >= upper_ends[:, None, :]).astype(jnp.int32), axis=2)
    valid = steps_all[None, :] < held_count[:, None]
    clipped = jnp.minimum(destination, N_PTS - 1)
    ranking = steps_all[None, :] - jnp.take_along_axis(starts, clipped, axis=1)
    before = jnp.cumsum(moved, axis=0) - moved
    spot_at = jnp.clip(jnp.take_along_axis(before, clipped, axis=1) + ranking, 0, PTS_DEV - 1)
    shuffles = jax.vmap(lambda subkey: jax.random.permutation(subkey, PTS_DEV))(jax.random.split(subkeys[7], N_PTS))
    places = clipped * PTS_DEV + shuffles[clipped, spot_at]
    slot_at = slot_index(ordering, held_count[:, None])
    result = jnp.full((N_PTS, OWN_CAP), -1, jnp.int32).at[devices[:, None], slot_at].set(jnp.where(valid, places, -1).astype(jnp.int32), mode='drop')
    return result.reshape(-1).astype(jnp.int32)


def draw_neighbors(key, part):
    subkeys, held_count, sent_counts, moved = layout(key)
    shape_all = (27, N_PTS, OWN_CAP)
    category = jax.random.randint(subkeys[8], shape_all, 0, 20)
    chosen = jax.random.randint(subkeys[9], shape_all, 0, jnp.broadcast_to(held_count[None, :, None], shape_all))
    rim_pick = jax.random.randint(subkeys[10], shape_all, 0, HALO)
    owner_of = jnp.arange(N_PTS)[None, :, None]
    column = jnp.arange(OWN_CAP)
    own_entry = HALO + slot_index(chosen, held_count[None, :, None])
    before = jnp.where(owner_of > 0, rim_pick, EXT_ROWS)
    after_entry = jnp.where(owner_of < N_PTS - 1, HALO + OWN_CAP + rim_pick, EXT_ROWS)
    entries = jnp.where(category < 7, EXT_ROWS, jnp.where(category < 14, own_entry, jnp.where(category < 17, before, after_entry)))
    entries = entries.at[13].set(jnp.broadcast_to(HALO + column[None, :], (N_PTS, OWN_CAP)))
    held_mask = jnp.logical_or(column[None, :] < held_count[:, None] - HALO, column[None, :] >= OWN_CAP - HALO)
    entries = jnp.where(held_mask[None], entries, EXT_ROWS)
    return entries.reshape(27, N_PTS * OWN_CAP).astype(jnp.int32)


def draw_qkv_bias(key, part):
    key_one = jax.random.fold_in(key, 0)
    baseline = jnp.clip(jax.random.normal(key_one, (3 * D,), jnp.float32) * 0.5, -2.0, 2.0)
    return baseline.astype(jnp.float32)


def block_levels(key, shape, pieces, low, largest):
    factor_of = 1.0
    for dim, parts in pieces:
        heights = jax.random.uniform(jax.random.fold_in(jax.random.fold_in(key, 6), dim), (parts,), jnp.float32, low / len(pieces), largest / len(pieces))
        factor_of = factor_of * jnp.repeat(jnp.exp(heights), shape[dim] // parts).reshape((-1,) + (1,) * (len(shape) - 1 - dim))
    return factor_of


def noise(stream_key, extent, width, bound, shards=(), dtype=jnp.bfloat16):
    array = jax.random.normal(stream_key, extent, jnp.float32) * width
    if len(shards) > 0:
        array = block_levels(stream_key, extent, shards, -0.22, 0.18) * array
    return jnp.clip(array, min=-bound, max=bound).astype(dtype)


def setup_inputs(seed: int = 0, part: int = 0) -> dict:
    key_list = jax.random.split(jax.random.key(seed), 15)
    own_keys = jax.random.split(jax.random.fold_in(key_list[14], part), 15)
    return {
        "features": noise(own_keys[0], (TOKENS, D), 1.0, 6.0, ((0, 8),)),
        "tile_slot": draw_tile_slot(jax.random.fold_in(jax.random.fold_in(key_list[14], part), 71), part),
        "neighbors": draw_neighbors(jax.random.fold_in(jax.random.fold_in(key_list[14], part), 71), part),
        "serial": draw_serial(jax.random.fold_in(jax.random.fold_in(key_list[14], part), 71), part),
        "conv_weight": noise(key_list[4], (27, D, D), (27 * D) ** -0.5, 0.078125),
        "conv_bias": noise(key_list[5], (D,), 0.5, 3.0, (), jnp.float32),
        "cpe_gain": jnp.clip(1.0 + 0.18 * jax.random.normal(key_list[6], (D,), jnp.float32), 0.1, 1.9),
        "cpe_bias": noise(key_list[7], (D,), 0.5, 3.0, (), jnp.float32),
        "norm_gain": jnp.clip(1.0 + 0.18 * jax.random.normal(key_list[8], (D,), jnp.float32), 0.1, 1.9),
        "norm_bias": noise(key_list[9], (D,), 0.5, 3.0, (), jnp.float32),
        "qkv_weight": noise(key_list[10], (D, 3 * D), D ** -0.5, 0.375),
        "qkv_bias": draw_qkv_bias(jax.random.fold_in(key_list[14], 71), part),
        "proj_weight": noise(key_list[12], (D, D), D ** -0.5, 0.375),
        "proj_bias": noise(key_list[13], (D,), 0.5, 3.0, (), jnp.float32),
    }


EPSILON = 1e-05

def layer_norm(values, gain_vec, shift_vec):
    average = lax.optimization_barrier(jnp.mean(values, axis=-1, keepdims=True))
    centred = values - average
    spread = lax.optimization_barrier(jnp.mean(centred * centred, axis=-1, keepdims=True))
    return centred * lax.rsqrt(spread + EPSILON) * gain_vec + shift_vec

def attend(qkv_rows, total_rows):
    patches = total_rows // PATCH

    def split_heads(matrix):
        return matrix.reshape(patches, PATCH, HEADS, HD).transpose(2, 0, 1, 3)
    query_heads = split_heads(qkv_rows[:, :D])
    key_heads = split_heads(qkv_rows[:, D:2 * D])
    value_heads = split_heads(qkv_rows[:, 2 * D:])

    def one_head(triple):
        query_h, key_h, value_h = triple
        scores = jnp.einsum('pqd,pkd->pqk', query_h.astype(jnp.float32), key_h.astype(jnp.float32)) * HD ** (-0.5)
        row_max = lax.optimization_barrier(jnp.max(scores, axis=-1, keepdims=True))
        lifted = jnp.exp(scores - row_max)
        row_sum = lax.optimization_barrier(jnp.sum(lifted, axis=-1, keepdims=True))
        weights = (lifted / row_sum).astype(jnp.bfloat16)
        return jnp.einsum('pqk,pkd->pqd', weights.astype(jnp.float32), value_h.astype(jnp.float32)).astype(jnp.bfloat16)
    heads_out = lax.map(one_head, (query_heads, key_heads, value_heads))
    return heads_out.transpose(1, 2, 0, 3).reshape(total_rows, D)

def reference(features, tile_slot, neighbors, serial, conv_weight, conv_bias, cpe_gain, cpe_bias, norm_gain, norm_bias, qkv_weight, qkv_bias, proj_weight, proj_bias):
    tiled_rows = jnp.zeros((TILE_ROWS, D), jnp.bfloat16).at[tile_slot].set(features)
    blocks = tiled_rows.reshape(N_PTS, OWN_CAP, D)
    rim_zero = jnp.zeros((1, HALO, D), jnp.bfloat16)
    before = jnp.concatenate([rim_zero, blocks[:-1, OWN_CAP - HALO:]], axis=0)
    after_rims = jnp.concatenate([blocks[1:, :HALO], rim_zero], axis=0)
    framed = jnp.concatenate([before, blocks, after_rims, jnp.zeros((N_PTS, 1, D), jnp.bfloat16)], axis=1)
    tables = neighbors.reshape(27, N_PTS, OWN_CAP).transpose(1, 0, 2)

    def owner_conv(paired):
        lookup, ext_rows = paired
        summed = jnp.zeros((OWN_CAP, D), jnp.float32)
        for offset in range(27):
            summed = summed + jnp.dot(ext_rows[lookup[offset]], conv_weight[offset], preferred_element_type=jnp.float32)
        return summed
    conv_out = lax.map(owner_conv, (tables, framed)).reshape(TILE_ROWS, D) + conv_bias
    hidden = (tiled_rows.astype(jnp.float32) + layer_norm(conv_out, cpe_gain, cpe_bias)).astype(jnp.bfloat16)
    target = jnp.where(serial >= 0, serial, TOKENS)
    placed = jnp.zeros((TOKENS, D), jnp.bfloat16).at[target].set(hidden, mode='drop')
    normed = layer_norm(placed.astype(jnp.float32), norm_gain, norm_bias).astype(jnp.bfloat16)
    qkv_rows = (jnp.dot(normed, qkv_weight, preferred_element_type=jnp.float32) + qkv_bias).astype(jnp.bfloat16)
    attended = attend(qkv_rows, TOKENS)
    projected = jnp.dot(attended, proj_weight, preferred_element_type=jnp.float32) + proj_bias
    return (placed.astype(jnp.float32) + projected).astype(jnp.bfloat16)
```

```python
import functools

import jax
import jax.numpy as jnp
from jax import lax
from jax.experimental import pallas as pl
from jax.experimental.pallas import tpu as pltpu
from jax.sharding import PartitionSpec as P

HEADS = 16
HD = 16
PATCH = 1024
PTS_DEV = 1024
OWN_CAP = 2048
HALO = 128
OFFSETS = 27
CENTRE = 13
CONV_BLOCK = 544
LANES = 128
QUERY_BLOCK = 256


EPSILON = 1e-05


def layer_norm(values, gain_vec, shift_vec):
    average = jnp.mean(values, axis=-1, keepdims=True)
    centred = values - average
    spread = jnp.mean(centred * centred, axis=-1, keepdims=True)
    return centred * lax.rsqrt(spread + EPSILON) * gain_vec + shift_vec


def arrival_rank(targets, wanted, num_peers):
    row_count = targets.shape[0]
    onehot = jnp.logical_and(targets[:, None] == jnp.arange(num_peers)[None, :], wanted[:, None])
    onehot_bf = onehot.astype(jnp.bfloat16)
    line = jnp.arange(row_count)
    lower = (line[None, :] < line[:, None]).astype(jnp.bfloat16)
    earlier = jnp.dot(lower, onehot_bf, preferred_element_type=jnp.float32)
    return jnp.sum(earlier * onehot.astype(jnp.float32), axis=1).astype(jnp.int32)


def buffer_index(targets, wanted, num_peers, stride, overflow):
    ranking = arrival_rank(targets, wanted, num_peers)
    return jnp.where(wanted, targets * stride + ranking, overflow)


def place_matrix(where_to, count):
    return (jnp.arange(count)[:, None] == where_to[None, :]).astype(jnp.bfloat16)


def place_rows(where_to, rows, count):
    return jnp.dot(
        place_matrix(where_to, count), rows, preferred_element_type=jnp.float32
    ).astype(jnp.bfloat16)


def place_numbers(where_to, numbers, missing, count):
    match = jnp.arange(count)[:, None] == where_to[None, :]
    return missing + jnp.sum(jnp.where(match, numbers[None, :] - missing, 0), axis=1)


def swap(values, num_peers):
    return lax.all_to_all(
        values.reshape((num_peers, -1) + values.shape[1:]),
        "pts",
        split_axis=0,
        concat_axis=0,
        tiled=True,
    ).reshape(values.shape)


def conv_kernel(
    block, table_ref, ext_ref, weight_ref, bias_ref, gain_ref, shift_ref,
    out_ref, rows_ref, pulled_ref, acc_ref,
):
    held = ext_ref.shape[0]

    @pl.when(pl.program_id(0) == 0)
    def _():
        chunk = 256

        def put(step, carry):
            base = pl.multiple_of(step * chunk, chunk)
            part = ext_ref[pl.ds(base, chunk), :].astype(jnp.float32)
            rows_ref[pl.ds(2 * base, chunk, stride=2), :] = part[:, :LANES]
            rows_ref[pl.ds(2 * base + 1, chunk, stride=2), :] = part[:, LANES:]
            return carry

        lax.fori_loop(0, held // chunk, put, 0)
        rows_ref[pl.ds(2 * held, 8), :] = jnp.zeros((8, LANES), jnp.float32)

    acc_ref[...] = jnp.zeros_like(acc_ref)

    def pull(offset):
        for row in range(block):
            at = pl.multiple_of(table_ref[0, 0, offset * block + row], 2)
            pulled_ref[pl.ds(2 * row, 2), :] = rows_ref[pl.ds(at, 2), :]

    def pulled_rows():
        return jnp.concatenate(
            [pulled_ref[pl.ds(0, block, stride=2), :], pulled_ref[pl.ds(1, block, stride=2), :]],
            axis=1,
        )

    def multiply(which):
        acc_ref[...] += jnp.dot(
            pulled_rows().astype(jnp.bfloat16),
            weight_ref[which],
            preferred_element_type=jnp.float32,
        )

    pull(0)

    def one(offset, carry):
        multiply(offset + (offset >= CENTRE).astype(jnp.int32))
        pull(offset + 1)
        return carry

    lax.fori_loop(0, OFFSETS - 1, one, 0)
    multiply(CENTRE)
    encoded = layer_norm(acc_ref[...] + bias_ref[...], gain_ref[...], shift_ref[...])
    out_ref[...] = (pulled_rows() + encoded).astype(jnp.bfloat16)


def conv_rows(table, extended, conv_weight, conv_bias, cpe_gain, cpe_bias):
    count = table.shape[1]
    block = CONV_BLOCK if count % CONV_BLOCK == 0 else count
    steps = count // block
    held, width = extended.shape
    lookup = table.reshape(OFFSETS, steps, block).transpose(1, 0, 2).reshape(
        steps, 1, OFFSETS * block
    )
    return pl.pallas_call(
        functools.partial(conv_kernel, block),
        grid=(steps,),
        out_shape=jax.ShapeDtypeStruct((count, width), jnp.bfloat16),
        in_specs=[
            pl.BlockSpec((1, 1, OFFSETS * block), lambda i: (i, 0, 0), memory_space=pltpu.SMEM)
        ]
        + [pl.BlockSpec(memory_space=pltpu.VMEM)] * 5,
        out_specs=pl.BlockSpec((block, width), lambda i: (i, 0)),
        scratch_shapes=[
            pltpu.VMEM((2 * held + 8, LANES), jnp.float32),
            pltpu.VMEM((2 * block, LANES), jnp.float32),
            pltpu.VMEM((block, width), jnp.float32),
        ],
        compiler_params=pltpu.CompilerParams(vmem_limit_bytes=32 * 2**20),
        cost_estimate=pl.CostEstimate(
            flops=2 * count * OFFSETS * width * width,
            bytes_accessed=conv_weight.size * 2 + count * width * 4,
            transcendentals=0,
        ),
    )(
        lookup, extended, conv_weight, conv_bias[None, :], cpe_gain[None, :], cpe_bias[None, :]
    )


def attend_kernel(
    got_ref, spots_ref, gain_ref, shift_ref, qkv_ref, qkv_bias_ref, proj_ref, proj_bias_ref,
    out_ref, placed_ref, heads_ref, attended_ref,
):
    rows, width = out_ref.shape
    size = QUERY_BLOCK
    for start in range(0, rows, size):
        line = lax.broadcasted_iota(jnp.int32, (size, 1), 0) + start
        match = jnp.where(spots_ref[...] == line, 1.0, 0.0).astype(jnp.bfloat16)
        placed = jnp.dot(match, got_ref[...], preferred_element_type=jnp.float32)
        placed_ref[pl.ds(start, size), :] = placed
        normed = layer_norm(placed, gain_ref[...], shift_ref[...]).astype(jnp.bfloat16)
        product = lax.dot_general(
            qkv_ref[...], normed, (((1,), (1,)), ((), ())), preferred_element_type=jnp.float32
        )
        heads_ref[:, pl.ds(start, size)] = (product + qkv_bias_ref[...]).astype(jnp.bfloat16)

    factor = HD ** (-0.5) * 1.4426950408889634

    def one_head(head, carry):
        base = pl.multiple_of(head * HD, HD)
        keys = heads_ref[pl.ds(width + base, HD), :]
        values = heads_ref[pl.ds(2 * width + base, HD), :]
        widened = jnp.concatenate([values, jnp.ones_like(values)], axis=0)
        for start in range(0, rows, size):
            queries = heads_ref[pl.ds(base, HD), pl.ds(start, size)]
            scores = lax.dot_general(
                keys, queries, (((0,), (0,)), ((), ())), preferred_element_type=jnp.float32
            )
            highest = jnp.max(scores, axis=0, keepdims=True)
            lifted = jnp.exp2((scores - highest) * factor).astype(jnp.bfloat16)
            summed = jnp.dot(widened, lifted, preferred_element_type=jnp.float32)
            attended_ref[pl.ds(base, HD), pl.ds(start, size)] = (
                summed[:HD] / summed[HD : HD + 1]
            ).astype(jnp.bfloat16)
        return carry

    lax.fori_loop(0, HEADS, one_head, 0)
    for start in range(0, rows, size):
        projected = lax.dot_general(
            attended_ref[:, pl.ds(start, size)],
            proj_ref[...],
            (((0,), (0,)), ((), ())),
            preferred_element_type=jnp.float32,
        )
        out_ref[pl.ds(start, size), :] = (
            placed_ref[pl.ds(start, size), :] + projected + proj_bias_ref[...]
        ).astype(jnp.bfloat16)


def attend_rows(
    got, spots, norm_gain, norm_bias, qkv_weight, qkv_bias, proj_weight, proj_bias, rows
):
    width = got.shape[1]
    return pl.pallas_call(
        attend_kernel,
        out_shape=jax.ShapeDtypeStruct((rows, width), jnp.bfloat16),
        in_specs=[pl.BlockSpec(memory_space=pltpu.VMEM)] * 8,
        out_specs=pl.BlockSpec(memory_space=pltpu.VMEM),
        scratch_shapes=[
            pltpu.VMEM((rows, width), jnp.float32),
            pltpu.VMEM((3 * width, rows), jnp.bfloat16),
            pltpu.VMEM((width, rows), jnp.bfloat16),
        ],
        compiler_params=pltpu.CompilerParams(vmem_limit_bytes=40 * 2**20),
    )(
        got, spots[None, :], norm_gain[None, :], norm_bias[None, :], qkv_weight.T,
        qkv_bias[:, None], proj_weight, proj_bias[None, :],
    )


def body(
    features,
    tile_slot,
    neighbors,
    serial,
    conv_weight,
    conv_bias,
    cpe_gain,
    cpe_bias,
    norm_gain,
    norm_bias,
    qkv_weight,
    qkv_bias,
    proj_weight,
    proj_bias,
):
    num_peers = lax.axis_size("pts")
    local_rows = features.shape[0]
    send_cap = 17 * local_rows // (8 * num_peers)
    total = num_peers * send_cap

    owners = tile_slot // OWN_CAP
    slot_in = tile_slot % OWN_CAP
    where_to = buffer_index(owners, jnp.ones(owners.shape, bool), num_peers, send_cap, total)
    got_slots = swap(place_numbers(where_to, slot_in, OWN_CAP, total), num_peers)
    got_rows = swap(place_rows(where_to, features, total), num_peers)
    line = jnp.arange(OWN_CAP)
    tiled_rows = jnp.dot(
        (line[:, None] == got_slots[None, :]).astype(jnp.bfloat16),
        got_rows,
        preferred_element_type=jnp.float32,
    ).astype(jnp.bfloat16)
    up = [(i, i + 1) for i in range(num_peers - 1)]
    down = [(i + 1, i) for i in range(num_peers - 1)]
    before = lax.ppermute(tiled_rows[OWN_CAP - HALO :], "pts", up)
    after = lax.ppermute(tiled_rows[:HALO], "pts", down)
    extended = jnp.concatenate([before, tiled_rows, after], axis=0)

    placed_ok = serial >= 0
    devices_to = jnp.where(placed_ok, serial // PTS_DEV, 0)
    where_to = buffer_index(devices_to, placed_ok, num_peers, send_cap, total)
    spots = place_numbers(where_to, serial % PTS_DEV, PTS_DEV, total)
    got_spots = swap(spots, num_peers)
    ordered = jnp.concatenate(
        [neighbors[:CENTRE], neighbors[CENTRE + 1 :], neighbors[CENTRE : CENTRE + 1]], axis=0
    )
    digits = jnp.concatenate([ordered // 64, ordered % 64], axis=0).astype(jnp.bfloat16)
    moved = lax.dot_general(
        digits,
        place_matrix(where_to, total),
        (((1,), (1,)), ((), ())),
        preferred_element_type=jnp.float32,
    )
    table = (moved[:OFFSETS] * 128 + moved[OFFSETS:] * 2).astype(jnp.int32)
    hidden = conv_rows(table, extended, conv_weight, conv_bias, cpe_gain, cpe_bias)
    got = swap(hidden, num_peers)
    return attend_rows(
        got, got_spots, norm_gain, norm_bias, qkv_weight, qkv_bias, proj_weight, proj_bias,
        local_rows,
    )


def solution(mesh):
    placed = (
        P(("dp", "pts"), None),
        P(("dp", "pts")),
        P(None, ("dp", "pts")),
        P(("dp", "pts")),
        P(),
        P(),
        P(),
        P(),
        P(),
        P(),
        P(),
        P(),
        P(),
        P(),
    )
    return jax.shard_map(
        body, mesh=mesh, in_specs=placed, out_specs=P(("dp", "pts"), None), check_vma=False
    )
```

```python
import functools

import jax
import jax.numpy as jnp
from jax import lax
from jax.experimental import pallas as pl
from jax.experimental.pallas import tpu as pltpu
from jax.sharding import PartitionSpec as P

HEADS = 16
HD = 16
PATCH = 1024
PTS_DEV = 1024
OWN_CAP = 2048
HALO = 128
OFFSETS = 27
CENTRE = 13
CONV_BLOCK = 768
FIRST_SHARE = (22, 34)
LANES = 128
ROW_BLOCK = 256


EPSILON = 1e-05


def layer_norm(values, gain_vec, shift_vec):
    average = jnp.mean(values, axis=-1, keepdims=True)
    centred = values - average
    spread = jnp.mean(centred * centred, axis=-1, keepdims=True)
    return centred * lax.rsqrt(spread + EPSILON) * gain_vec + shift_vec


def arrival_rank(targets, wanted, num_peers):
    row_count = targets.shape[0]
    onehot = jnp.logical_and(targets[:, None] == jnp.arange(num_peers)[None, :], wanted[:, None])
    onehot_bf = onehot.astype(jnp.bfloat16)
    line = jnp.arange(row_count)
    lower = (line[None, :] < line[:, None]).astype(jnp.bfloat16)
    earlier = jnp.dot(lower, onehot_bf, preferred_element_type=jnp.float32)
    return jnp.sum(earlier * onehot.astype(jnp.float32), axis=1).astype(jnp.int32)


def buffer_index(targets, wanted, num_peers, stride, overflow):
    ranking = arrival_rank(targets, wanted, num_peers)
    return jnp.where(wanted, targets * stride + ranking, overflow)


def place_matrix(where_to, count):
    return (jnp.arange(count)[:, None] == where_to[None, :]).astype(jnp.bfloat16)


def place_rows(where_to, rows, count):
    return jnp.dot(
        place_matrix(where_to, count), rows, preferred_element_type=jnp.float32
    ).astype(jnp.bfloat16)


def place_numbers(where_to, numbers, missing, count):
    match = jnp.arange(count)[:, None] == where_to[None, :]
    return missing + jnp.sum(jnp.where(match, numbers[None, :] - missing, 0), axis=1)


def swap(values, num_peers):
    return lax.all_to_all(
        values.reshape((num_peers, -1) + values.shape[1:]),
        "pts",
        split_axis=0,
        concat_axis=0,
        tiled=True,
    ).reshape(values.shape)


def conv_kernel(
    block, table_ref, ext_ref, weight_ref, bias_ref, gain_ref, shift_ref,
    out_ref, rows_ref, pulled_ref, acc_ref,
):
    held = ext_ref.shape[0]

    @pl.when(pl.program_id(0) == 0)
    def _():
        chunk = 256

        def put(step, carry):
            base = pl.multiple_of(step * chunk, chunk)
            part = ext_ref[pl.ds(base, chunk), :].astype(jnp.float32)
            rows_ref[pl.ds(2 * base, chunk, stride=2), :] = part[:, :LANES]
            rows_ref[pl.ds(2 * base + 1, chunk, stride=2), :] = part[:, LANES:]
            return carry

        lax.fori_loop(0, held // chunk, put, 0)
        rows_ref[pl.ds(2 * held, 8), :] = jnp.zeros((8, LANES), jnp.float32)

    acc_ref[...] = jnp.zeros_like(acc_ref)

    def pull(offset):
        for row in range(block):
            at = pl.multiple_of(table_ref[0, 0, offset * block + row], 2)
            pulled_ref[pl.ds(2 * row, 2), :] = rows_ref[pl.ds(at, 2), :]

    def pulled_rows():
        return jnp.concatenate(
            [pulled_ref[pl.ds(0, block, stride=2), :], pulled_ref[pl.ds(1, block, stride=2), :]],
            axis=1,
        )

    def multiply(which):
        acc_ref[...] += jnp.dot(
            pulled_rows().astype(jnp.bfloat16),
            weight_ref[which],
            preferred_element_type=jnp.float32,
        )

    pull(0)

    def one(offset, carry):
        multiply(offset + (offset >= CENTRE).astype(jnp.int32))
        pull(offset + 1)
        return carry

    lax.fori_loop(0, OFFSETS - 1, one, 0)
    multiply(CENTRE)
    encoded = layer_norm(acc_ref[...] + bias_ref[...], gain_ref[...], shift_ref[...])
    out_ref[...] = (pulled_rows() + encoded).astype(jnp.bfloat16)


def conv_rows(table, extended, conv_weight, conv_bias, cpe_gain, cpe_bias):
    count = table.shape[1]
    steps = -(-count // CONV_BLOCK)
    block = count // steps
    held, width = extended.shape
    lookup = table.reshape(OFFSETS, steps, block).transpose(1, 0, 2).reshape(
        steps, 1, OFFSETS * block
    )
    return pl.pallas_call(
        functools.partial(conv_kernel, block),
        grid=(steps,),
        out_shape=jax.ShapeDtypeStruct((count, width), jnp.bfloat16),
        in_specs=[
            pl.BlockSpec((1, 1, OFFSETS * block), lambda i: (i, 0, 0), memory_space=pltpu.SMEM)
        ]
        + [pl.BlockSpec(memory_space=pltpu.VMEM)] * 5,
        out_specs=pl.BlockSpec((block, width), lambda i: (i, 0)),
        scratch_shapes=[
            pltpu.VMEM((2 * held + 8, LANES), jnp.float32),
            pltpu.VMEM((2 * block, LANES), jnp.float32),
            pltpu.VMEM((block, width), jnp.float32),
        ],
        compiler_params=pltpu.CompilerParams(vmem_limit_bytes=32 * 2**20),
        cost_estimate=pl.CostEstimate(
            flops=2 * count * OFFSETS * width * width,
            bytes_accessed=conv_weight.size * 2 + count * width * 4,
            transcendentals=0,
        ),
    )(
        lookup, extended, conv_weight, conv_bias[None, :], cpe_gain[None, :], cpe_bias[None, :]
    )


def attend_kernel(
    first_ref, last_ref, first_spots_ref, last_spots_ref, gain_ref, shift_ref, qkv_ref, qkv_bias_ref,
    proj_ref, proj_bias_ref, out_ref, placed_ref, heads_ref, attended_ref,
):
    rows, width = out_ref.shape
    size = ROW_BLOCK
    for start in range(0, rows, size):
        line = lax.broadcasted_iota(jnp.int32, (size, 1), 0) + start
        placed = 0.0
        for got_ref, spots_ref in ((first_ref, first_spots_ref), (last_ref, last_spots_ref)):
            match = jnp.where(spots_ref[...] == line, 1.0, 0.0).astype(jnp.bfloat16)
            placed += jnp.dot(match, got_ref[...], preferred_element_type=jnp.float32)
        placed_ref[pl.ds(start, size), :] = placed
        normed = layer_norm(placed, gain_ref[...], shift_ref[...]).astype(jnp.bfloat16)
        product = lax.dot_general(
            qkv_ref[...], normed, (((1,), (1,)), ((), ())), preferred_element_type=jnp.float32
        )
        heads_ref[:, pl.ds(start, size)] = (product + qkv_bias_ref[...]).astype(jnp.bfloat16)

    factor = HD ** (-0.5) * 1.4426950408889634

    def one_head(head, carry):
        base = pl.multiple_of(head * HD, HD)
        keys = heads_ref[pl.ds(width + base, HD), :]
        values = heads_ref[pl.ds(2 * width + base, HD), :]
        widened = jnp.concatenate([values, jnp.ones_like(values)], axis=0)
        queries = heads_ref[pl.ds(base, HD), :]
        scores = jnp.dot(keys.T, queries, preferred_element_type=jnp.float32)
        highest = jnp.max(scores, axis=0, keepdims=True)
        lifted = jnp.exp2((scores - highest) * factor).astype(jnp.bfloat16)
        summed = jnp.dot(widened, lifted, preferred_element_type=jnp.float32)
        attended_ref[pl.ds(base, HD), :] = (summed[:HD] / summed[HD : HD + 1]).astype(jnp.bfloat16)
        return carry

    lax.fori_loop(0, HEADS, one_head, 0, unroll=4)
    for start in range(0, rows, size):
        projected = lax.dot_general(
            attended_ref[:, pl.ds(start, size)],
            proj_ref[...],
            (((0,), (0,)), ((), ())),
            preferred_element_type=jnp.float32,
        )
        out_ref[pl.ds(start, size), :] = (
            placed_ref[pl.ds(start, size), :] + projected + proj_bias_ref[...]
        ).astype(jnp.bfloat16)


def attend_rows(
    first, last, first_spots, last_spots, norm_gain, norm_bias, qkv_weight, qkv_bias,
    proj_weight, proj_bias, rows,
):
    width = first.shape[1]
    return pl.pallas_call(
        attend_kernel,
        out_shape=jax.ShapeDtypeStruct((rows, width), jnp.bfloat16),
        in_specs=[pl.BlockSpec(memory_space=pltpu.VMEM)] * 10,
        out_specs=pl.BlockSpec(memory_space=pltpu.VMEM),
        scratch_shapes=[
            pltpu.VMEM((rows, width), jnp.float32),
            pltpu.VMEM((3 * width, rows), jnp.bfloat16),
            pltpu.VMEM((width, rows), jnp.bfloat16),
        ],
        compiler_params=pltpu.CompilerParams(vmem_limit_bytes=50 * 2**20),
    )(
        first, last, first_spots[None, :], last_spots[None, :], norm_gain[None, :], norm_bias[None, :], qkv_weight.T,
        qkv_bias[:, None], proj_weight, proj_bias[None, :],
    )


def body(
    features,
    tile_slot,
    neighbors,
    serial,
    conv_weight,
    conv_bias,
    cpe_gain,
    cpe_bias,
    norm_gain,
    norm_bias,
    qkv_weight,
    qkv_bias,
    proj_weight,
    proj_bias,
):
    num_peers = lax.axis_size("pts")
    local_rows = features.shape[0]
    send_cap = 17 * local_rows // (8 * num_peers)
    total = num_peers * send_cap

    owners = tile_slot // OWN_CAP
    where_to = buffer_index(owners, jnp.ones(owners.shape, bool), num_peers, send_cap, total)
    packed, serial, where_in = lax.optimization_barrier(
        (place_rows(where_to, features, total), serial, where_to)
    )
    got_rows = swap(packed, num_peers)
    slots = place_numbers(where_in, tile_slot % OWN_CAP, OWN_CAP, total)

    cap_first = send_cap * FIRST_SHARE[0] // FIRST_SHARE[1]
    cap_last = send_cap - cap_first
    count_first = num_peers * cap_first
    placed_ok = serial >= 0
    devices_to = jnp.where(placed_ok, serial // PTS_DEV, 0)
    ranking = arrival_rank(devices_to, placed_ok, num_peers)
    where_to = jnp.where(placed_ok, devices_to * send_cap + ranking, total)
    spots = place_numbers(where_to, serial % PTS_DEV, PTS_DEV, total)
    numbers = lax.all_to_all(
        jnp.concatenate(
            [slots.reshape(num_peers, send_cap), spots.reshape(num_peers, send_cap)], axis=1
        ),
        "pts",
        split_axis=0,
        concat_axis=0,
        tiled=True,
    )
    got_slots = numbers[:, :send_cap].reshape(-1)
    first_spots = numbers[:, send_cap : send_cap + cap_first].reshape(-1)
    last_spots = numbers[:, send_cap + cap_first :].reshape(-1)

    order = jnp.where(
        ranking < cap_first,
        devices_to * cap_first + ranking,
        count_first + devices_to * cap_last + ranking - cap_first,
    )
    order = jnp.where(placed_ok, order, total)
    ordered = jnp.concatenate(
        [neighbors[:CENTRE], neighbors[CENTRE + 1 :], neighbors[CENTRE : CENTRE + 1]], axis=0
    )
    digits = jnp.concatenate([ordered // 64, ordered % 64], axis=0).astype(jnp.bfloat16)
    moved = lax.dot_general(
        digits,
        place_matrix(order, total),
        (((1,), (1,)), ((), ())),
        preferred_element_type=jnp.float32,
    )
    table = (moved[:OFFSETS] * 128 + moved[OFFSETS:] * 2).astype(jnp.int32)

    def lay(lines):
        return jnp.dot(
            (lines[:, None] == got_slots[None, :]).astype(jnp.bfloat16),
            got_rows,
            preferred_element_type=jnp.float32,
        ).astype(jnp.bfloat16)

    up = [(i, i + 1) for i in range(num_peers - 1)]
    down = [(i + 1, i) for i in range(num_peers - 1)]
    before = lax.ppermute(lay(jnp.arange(OWN_CAP - HALO, OWN_CAP)), "pts", up)
    after = lax.ppermute(lay(jnp.arange(HALO)), "pts", down)
    extended = jnp.concatenate([before, lay(jnp.arange(OWN_CAP)), after], axis=0)

    weights = (conv_weight, conv_bias, cpe_gain, cpe_bias)
    first = conv_rows(table[:, :count_first], extended, *weights)
    first, later = lax.optimization_barrier((first, table[:, count_first:]))
    first = swap(first, num_peers)
    last = swap(conv_rows(later, extended, *weights), num_peers)
    return attend_rows(
        first, last, first_spots, last_spots, norm_gain, norm_bias, qkv_weight, qkv_bias,
        proj_weight, proj_bias, local_rows,
    )


def solution(mesh):
    placed = (
        P(("dp", "pts"), None),
        P(("dp", "pts")),
        P(None, ("dp", "pts")),
        P(("dp", "pts")),
        P(),
        P(),
        P(),
        P(),
        P(),
        P(),
        P(),
        P(),
        P(),
        P(),
    )
    return jax.shard_map(
        body, mesh=mesh, in_specs=placed, out_specs=P(("dp", "pts"), None), check_vma=False
    )
```

```python
import functools

import jax
import jax.numpy as jnp
from jax import lax
from jax.experimental import pallas as pl
from jax.experimental.pallas import tpu as pltpu
from jax.sharding import PartitionSpec as P

HEADS = 16
HD = 16
PATCH = 1024
PTS_DEV = 1024
OWN_CAP = 2048
HALO = 128
OFFSETS = 27
CENTRE = 13
CONV_BLOCK = 1088
LANES = 128
ROW_BLOCK = 256


EPSILON = 1e-05


def layer_norm(values, gain_vec, shift_vec):
    average = jnp.mean(values, axis=-1, keepdims=True)
    centred = values - average
    spread = jnp.mean(centred * centred, axis=-1, keepdims=True)
    return centred * lax.rsqrt(spread + EPSILON) * gain_vec + shift_vec


def arrival_rank(targets, wanted, num_peers):
    row_count = targets.shape[0]
    onehot = jnp.logical_and(targets[:, None] == jnp.arange(num_peers)[None, :], wanted[:, None])
    onehot_bf = onehot.astype(jnp.bfloat16)
    line = jnp.arange(row_count)
    lower = (line[None, :] < line[:, None]).astype(jnp.bfloat16)
    earlier = jnp.dot(lower, onehot_bf, preferred_element_type=jnp.float32)
    return jnp.sum(earlier * onehot.astype(jnp.float32), axis=1).astype(jnp.int32)


def buffer_index(targets, wanted, num_peers, stride, overflow):
    ranking = arrival_rank(targets, wanted, num_peers)
    return jnp.where(wanted, targets * stride + ranking, overflow)


def place_matrix(where_to, count):
    return (jnp.arange(count)[:, None] == where_to[None, :]).astype(jnp.bfloat16)


def place_rows(where_to, rows, count):
    return jnp.dot(
        place_matrix(where_to, count), rows, preferred_element_type=jnp.float32
    ).astype(jnp.bfloat16)


def place_numbers(where_to, numbers, missing, count):
    match = jnp.arange(count)[:, None] == where_to[None, :]
    return missing + jnp.sum(jnp.where(match, numbers[None, :] - missing, 0), axis=1)


def swap(values, num_peers):
    return lax.all_to_all(
        values.reshape((num_peers, -1) + values.shape[1:]),
        "pts",
        split_axis=0,
        concat_axis=0,
        tiled=True,
    ).reshape(values.shape)


def conv_kernel(
    block, table_ref, ext_ref, weight_ref, bias_ref, gain_ref, shift_ref,
    out_ref, rows_ref, pulled_ref, acc_ref,
):
    held = ext_ref.shape[0]

    @pl.when(pl.program_id(0) == 0)
    def _():
        chunk = 256

        def put(step, carry):
            base = pl.multiple_of(step * chunk, chunk)
            part = ext_ref[pl.ds(base, chunk), :].astype(jnp.float32)
            rows_ref[pl.ds(2 * base, chunk, stride=2), :] = part[:, :LANES]
            rows_ref[pl.ds(2 * base + 1, chunk, stride=2), :] = part[:, LANES:]
            return carry

        lax.fori_loop(0, held // chunk, put, 0)
        rows_ref[pl.ds(2 * held, 8), :] = jnp.zeros((8, LANES), jnp.float32)

    acc_ref[...] = jnp.zeros_like(acc_ref)

    def pull(offset):
        for row in range(block):
            at = pl.multiple_of(table_ref[0, 0, offset * block + row], 2)
            pulled_ref[pl.ds(2 * row, 2), :] = rows_ref[pl.ds(at, 2), :]

    def pulled_rows():
        return jnp.concatenate(
            [pulled_ref[pl.ds(0, block, stride=2), :], pulled_ref[pl.ds(1, block, stride=2), :]],
            axis=1,
        )

    def multiply(which):
        acc_ref[...] += jnp.dot(
            pulled_rows().astype(jnp.bfloat16),
            weight_ref[which],
            preferred_element_type=jnp.float32,
        )

    pull(0)

    def one(offset, carry):
        multiply(offset + (offset >= CENTRE).astype(jnp.int32))
        pull(offset + 1)
        return carry

    lax.fori_loop(0, OFFSETS - 1, one, 0)
    multiply(CENTRE)
    encoded = layer_norm(acc_ref[...] + bias_ref[...], gain_ref[...], shift_ref[...])
    out_ref[...] = (pulled_rows() + encoded).astype(jnp.bfloat16)


def conv_rows(table, extended, conv_weight, conv_bias, cpe_gain, cpe_bias):
    count = table.shape[1]
    steps = -(-count // CONV_BLOCK)
    block = count // steps
    held, width = extended.shape
    lookup = table.reshape(OFFSETS, steps, block).transpose(1, 0, 2).reshape(
        steps, 1, OFFSETS * block
    )
    return pl.pallas_call(
        functools.partial(conv_kernel, block),
        grid=(steps,),
        out_shape=jax.ShapeDtypeStruct((count, width), jnp.bfloat16),
        in_specs=[
            pl.BlockSpec((1, 1, OFFSETS * block), lambda i: (i, 0, 0), memory_space=pltpu.SMEM)
        ]
        + [pl.BlockSpec(memory_space=pltpu.VMEM)] * 5,
        out_specs=pl.BlockSpec((block, width), lambda i: (i, 0)),
        scratch_shapes=[
            pltpu.VMEM((2 * held + 8, LANES), jnp.float32),
            pltpu.VMEM((2 * block, LANES), jnp.float32),
            pltpu.VMEM((block, width), jnp.float32),
        ],
        compiler_params=pltpu.CompilerParams(vmem_limit_bytes=32 * 2**20),
        cost_estimate=pl.CostEstimate(
            flops=2 * count * OFFSETS * width * width,
            bytes_accessed=conv_weight.size * 2 + count * width * 4,
            transcendentals=0,
        ),
    )(
        lookup, extended, conv_weight, conv_bias[None, :], cpe_gain[None, :], cpe_bias[None, :]
    )


def attend_kernel(
    got_ref, spots_ref, gain_ref, shift_ref, qkv_ref, qkv_bias_ref,
    proj_ref, proj_bias_ref, out_ref, placed_ref, heads_ref, attended_ref,
):
    rows, width = out_ref.shape
    size = ROW_BLOCK
    for start in range(0, rows, size):
        line = lax.broadcasted_iota(jnp.int32, (size, 1), 0) + start
        match = jnp.where(spots_ref[...] == line, 1.0, 0.0).astype(jnp.bfloat16)
        placed = jnp.dot(match, got_ref[...], preferred_element_type=jnp.float32)
        placed_ref[pl.ds(start, size), :] = placed
        normed = layer_norm(placed, gain_ref[...], shift_ref[...]).astype(jnp.bfloat16)
        product = lax.dot_general(
            qkv_ref[...], normed, (((1,), (1,)), ((), ())), preferred_element_type=jnp.float32
        )
        heads_ref[:, pl.ds(start, size)] = (product + qkv_bias_ref[...]).astype(jnp.bfloat16)

    factor = HD ** (-0.5) * 1.4426950408889634

    def one_head(head, carry):
        base = pl.multiple_of(head * HD, HD)
        keys = heads_ref[pl.ds(width + base, HD), :]
        values = heads_ref[pl.ds(2 * width + base, HD), :]
        widened = jnp.concatenate([values, jnp.ones_like(values)], axis=0)
        queries = heads_ref[pl.ds(base, HD), :]
        scores = jnp.dot(keys.T, queries, preferred_element_type=jnp.float32)
        highest = jnp.max(scores, axis=0, keepdims=True)
        lifted = jnp.exp2((scores - highest) * factor).astype(jnp.bfloat16)
        summed = jnp.dot(widened, lifted, preferred_element_type=jnp.float32)
        attended_ref[pl.ds(base, HD), :] = (summed[:HD] / summed[HD : HD + 1]).astype(jnp.bfloat16)
        return carry

    lax.fori_loop(0, HEADS, one_head, 0, unroll=4)
    for start in range(0, rows, size):
        projected = lax.dot_general(
            attended_ref[:, pl.ds(start, size)],
            proj_ref[...],
            (((0,), (0,)), ((), ())),
            preferred_element_type=jnp.float32,
        )
        out_ref[pl.ds(start, size), :] = (
            placed_ref[pl.ds(start, size), :] + projected + proj_bias_ref[...]
        ).astype(jnp.bfloat16)


def attend_rows(
    got, spots, norm_gain, norm_bias, qkv_weight, qkv_bias, proj_weight, proj_bias, rows
):
    width = got.shape[1]
    return pl.pallas_call(
        attend_kernel,
        out_shape=jax.ShapeDtypeStruct((rows, width), jnp.bfloat16),
        in_specs=[pl.BlockSpec(memory_space=pltpu.VMEM)] * 8,
        out_specs=pl.BlockSpec(memory_space=pltpu.VMEM),
        scratch_shapes=[
            pltpu.VMEM((rows, width), jnp.float32),
            pltpu.VMEM((3 * width, rows), jnp.bfloat16),
            pltpu.VMEM((width, rows), jnp.bfloat16),
        ],
        compiler_params=pltpu.CompilerParams(vmem_limit_bytes=50 * 2**20),
    )(
        got, spots[None, :], norm_gain[None, :], norm_bias[None, :], qkv_weight.T,
        qkv_bias[:, None], proj_weight, proj_bias[None, :],
    )


def body(
    features,
    tile_slot,
    neighbors,
    serial,
    conv_weight,
    conv_bias,
    cpe_gain,
    cpe_bias,
    norm_gain,
    norm_bias,
    qkv_weight,
    qkv_bias,
    proj_weight,
    proj_bias,
):
    num_peers = lax.axis_size("pts")
    local_rows = features.shape[0]
    send_cap = 17 * local_rows // (8 * num_peers)
    total = num_peers * send_cap

    owners = tile_slot // OWN_CAP
    where_to = buffer_index(owners, jnp.ones(owners.shape, bool), num_peers, send_cap, total)
    got_rows = swap(place_rows(where_to, features, total), num_peers)
    slots = place_numbers(where_to, tile_slot % OWN_CAP, OWN_CAP, total)

    placed_ok = serial >= 0
    devices_to = jnp.where(placed_ok, serial // PTS_DEV, 0)
    where_to = buffer_index(devices_to, placed_ok, num_peers, send_cap, total)
    spots = place_numbers(where_to, serial % PTS_DEV, PTS_DEV, total)
    numbers = lax.all_to_all(
        jnp.concatenate(
            [slots.reshape(num_peers, send_cap), spots.reshape(num_peers, send_cap)], axis=1
        ),
        "pts",
        split_axis=0,
        concat_axis=0,
        tiled=True,
    )
    got_slots = numbers[:, :send_cap].reshape(-1)
    got_spots = numbers[:, send_cap:].reshape(-1)
    ordered = jnp.concatenate(
        [neighbors[:CENTRE], neighbors[CENTRE + 1 :], neighbors[CENTRE : CENTRE + 1]], axis=0
    )
    digits = jnp.concatenate([ordered // 64, ordered % 64], axis=0).astype(jnp.bfloat16)
    moved = lax.dot_general(
        digits,
        place_matrix(where_to, total),
        (((1,), (1,)), ((), ())),
        preferred_element_type=jnp.float32,
    )
    table = (moved[:OFFSETS] * 128 + moved[OFFSETS:] * 2).astype(jnp.int32)

    def lay(lines):
        return jnp.dot(
            (lines[:, None] == got_slots[None, :]).astype(jnp.bfloat16),
            got_rows,
            preferred_element_type=jnp.float32,
        ).astype(jnp.bfloat16)

    up = [(i, i + 1) for i in range(num_peers - 1)]
    down = [(i + 1, i) for i in range(num_peers - 1)]
    before = lax.ppermute(lay(jnp.arange(OWN_CAP - HALO, OWN_CAP)), "pts", up)
    after = lax.ppermute(lay(jnp.arange(HALO)), "pts", down)
    extended = jnp.concatenate([before, lay(jnp.arange(OWN_CAP)), after], axis=0)

    hidden = conv_rows(table, extended, conv_weight, conv_bias, cpe_gain, cpe_bias)
    got = swap(hidden, num_peers)
    return attend_rows(
        got, got_spots, norm_gain, norm_bias, qkv_weight, qkv_bias, proj_weight, proj_bias,
        local_rows,
    )


def solution(mesh):
    placed = (
        P(("dp", "pts"), None),
        P(("dp", "pts")),
        P(None, ("dp", "pts")),
        P(("dp", "pts")),
        P(),
        P(),
        P(),
        P(),
        P(),
        P(),
        P(),
        P(),
        P(),
        P(),
    )
    return jax.shard_map(
        body, mesh=mesh, in_specs=placed, out_specs=P(("dp", "pts"), None), check_vma=False
    )
```
